256 devices in a mesh: frame: 32 (over x, z_hi, core), pix: 8 (over z_lo, y).
Axes of the slice: x: 4, y: 4, z: 8 (z_hi: 4, z_lo: 2; z = z_hi * 2 + z_lo), core: 2. Of those that a mesh axis runs over, the one named last changes fastest.
Arguments:
- frames: float32 [16384, 16384], P('frame', 'pix'), may hold values from 2 to 42, as said below
- dark: float32 [16384], P('pix'), may hold values from 0.5 to 1.9
Outputs:
- two_time: float32 [512, 32, 8, 512], P('pix', 'frame')
The draws below stay inside these ranges and needn't reach their ends.
Inputs may be any that keep to these rules, and one draw needn't show every extreme that they name: `frames`: every frame count exceeds every dark level by a positive signal.
All inputs are finite; a program needn't handle non-finite values.
Results may differ from the reference program's by a relative error of at most 0.0003.
Values may be sent and summed in bfloat16 or wider, within the bound.
A program may use at most 128 MiB of HBM per device.

```python
import jax
import jax.numpy as jnp
from jax import lax

BS = 512
BAND = 8
PIX = 16384
NB = 32
EXPOSURE_SUM = 16384


def draw_frames(key, part):
    key = jax.random.fold_in(key, 11)
    stochastic_seed_keys = jax.random.split(key, 8)
    grain_number = min(PIX, 512)
    grain_width = PIX // grain_number
    hold_shift = jax.random.randint(stochastic_seed_keys[0], (grain_number,), 0, 8)
    hold_frames = jnp.maximum(jnp.left_shift(jnp.full((grain_number,), BS, jnp.int32), hold_shift) // 16, 1)
    jump_limit = (1 << 20) // hold_frames
    jump_draws = jax.random.randint(stochastic_seed_keys[1], (EXPOSURE_SUM, grain_number), 0, 1 << 20)
    uniform_stride = jump_draws < jump_limit[None, :]
    episode_exposures = jax.random.randint(stochastic_seed_keys[2], (6,), 1, EXPOSURE_SUM)
    exposure_ordinal = jnp.arange(EXPOSURE_SUM, dtype=jnp.int32)
    within_episode = jnp.any(exposure_ordinal[:, None] == episode_exposures[None, :], axis=1)
    episode_choice_mask = jax.random.randint(stochastic_seed_keys[3], (EXPOSURE_SUM, grain_number), 0, 2) == 1
    stride_flags = (uniform_stride | within_episode[:, None] & episode_choice_mask) & (exposure_ordinal[:, None] > 0)
    segment = jnp.cumsum(stride_flags.astype(jnp.int32), axis=0)
    level_table = jax.random.uniform(stochastic_seed_keys[4], (EXPOSURE_SUM, grain_number), jnp.float32)
    grain_level = jnp.take_along_axis(level_table, segment, axis=0)
    bright = grain_level ** 8
    own_factor = jax.random.uniform(stochastic_seed_keys[5], (EXPOSURE_SUM, PIX), jnp.float32, 0.5, 1.0)
    gain_exponent = jax.random.uniform(stochastic_seed_keys[6], (PIX,), jnp.float32, 0.0, 0.75)
    pixel_trend = jax.random.uniform(stochastic_seed_keys[7], (PIX,), jnp.float32, -0.125, 0.125)
    times_frac = jnp.arange(EXPOSURE_SUM, dtype=jnp.float32) / (EXPOSURE_SUM - 1)
    pixel_gain = 10.0 ** (-gain_exponent[None, :] - 0.125 + pixel_trend[None, :] * (2.0 * times_frac[:, None] - 1.0))
    spread_bright = jnp.repeat(bright, grain_width, axis=1)
    return (2.0 + 40.0 * pixel_gain * spread_bright * own_factor).astype(jnp.float32)


def level_of(own_key, shape, cuts, least, largest):
    loudness = 1.0
    for dim, parts in cuts:
        draws = jax.random.uniform(jax.random.fold_in(jax.random.fold_in(own_key, 6), dim), (parts,), jnp.float32, least / len(cuts), largest / len(cuts))
        loudness = loudness * jnp.repeat(jnp.exp(draws), shape[dim] // parts).reshape((-1,) + (1,) * (len(shape) - 1 - dim))
    return loudness


def setup_inputs(seed: int = 0) -> dict:
    key_list = jax.random.split(jax.random.key(seed), 3)
    return {
        "frames": draw_frames(jax.random.fold_in(key_list[2], 71), 0),
        "dark": jnp.clip(0.5 + 1.4 * jax.random.uniform(key_list[1], (PIX,), jnp.float32) ** level_of(key_list[1], (PIX,), ((0, 8),), -0.2, 0.2), 0.5, 1.9),
    }


def reference(frames, dark):
    signal = frames - dark[None, :]
    pixel_mean = jnp.sum(signal, axis=0) / EXPOSURE_SUM
    normalized = (signal / pixel_mean[None, :]).astype(jnp.bfloat16)
    frame_mean = jnp.sum(normalized, axis=1, dtype=jnp.float32) / PIX
    padded = jnp.concatenate([normalized, jnp.zeros(((BAND - 1) * BS, PIX), jnp.bfloat16)], axis=0)
    padded_mean = jnp.concatenate([frame_mean, jnp.ones(((BAND - 1) * BS,), jnp.float32)], axis=0)

    def one_block(block_idx):
        left_rows = lax.dynamic_slice_in_dim(normalized, block_idx * BS, BS, 0)
        right_rows = lax.dynamic_slice_in_dim(padded, block_idx * BS, BAND * BS, 0)
        gram_sums = lax.dot_general(left_rows, right_rows, (((1,), (1,)), ((), ())), preferred_element_type=jnp.float32)
        gram_sums = gram_sums.reshape(BS, BAND, BS)
        left_mean = lax.dynamic_slice_in_dim(frame_mean, block_idx * BS, BS, 0)
        right_mean = lax.dynamic_slice_in_dim(padded_mean, block_idx * BS, BAND * BS, 0).reshape(BAND, BS)
        lag_index = jnp.arange(BAND, dtype=jnp.int32)
        in_band = (block_idx + lag_index < NB)[None, :, None]
        result = gram_sums / (PIX * left_mean[:, None, None] * right_mean[None, :, :])
        return jnp.where(in_band, result, jnp.zeros_like(result))

    blocks_all = lax.map(one_block, jnp.arange(NB, dtype=jnp.int32))
    return jnp.transpose(blocks_all, (1, 0, 2, 3))
```

```python
import functools

import jax
import jax.numpy as jnp
from jax import lax
from jax.experimental import pallas as pl
from jax.experimental.pallas import tpu as pltpu
from jax.sharding import PartitionSpec as P

BS = 512
CR = 128
T = BS // CR
BAND = 8
F32 = jnp.float32
BF16 = jnp.bfloat16
MESH = pl.DeviceIdType.MESH


def nt_dot(left, right):
    return lax.dot_general(left, right, (((1,), (1,)), ((), ())), preferred_element_type=F32)


def kernel(total_frames, total_pix, frames, dark, out,
           fr, a, aw, ap, nx, th, ex, nw, ys, yr, zs, zo, zr, shs, shr,
           cs, cr, winv, fs, fy, fz, fmr, fcol,
           fl_s, x_s, x_r, dn_s, dn_r, up_s, up_r, ce_s, ce_r, cn_s, cn_r, ct_s, ct_r,
           ys_s, ys_r, zs_s, zs_r, sh_s, sh_r, cs_s, cs_r, fy_s, fy_r, fz_s, fz_r, fm_s, fm_r):
    f = lax.axis_index("frame")
    p = lax.axis_index("pix")
    nf = 32
    c = lax.rem(f, 2)
    k = f // 2
    z = lax.rem(k, 4)
    x = k // 4
    y = lax.rem(p, 4)
    zl = p // 4

    def fdev(nx_, nz_, nc_):
        return ((nx_ * 4 + nz_) * 2 + nc_, p)

    def fwrap(d):
        return (lax.rem(f + d + nf, nf), p)

    def zdev(o):
        return fdev(x, lax.rem(z + o, 4), c)

    def xdev(o):
        return fdev(lax.rem(x + o, 4), z, c)

    def ydev(o):
        return (f, zl * 4 + lax.rem(y + o, 4))

    core = fdev(x, z, 1 - c)
    zpartner = (f, (1 - zl) * 4 + y)

    barrier = pltpu.get_barrier_semaphore()
    greet = [core, zpartner]
    greet += [zdev(o) for o in (1, 2, 3)]
    greet += [xdev(o) for o in (1, 2, 3)]
    greet += [ydev(o) for o in (1, 2, 3)]
    greet += [fwrap(d) for d in range(1, 8)]
    greet += [fwrap(-2)]
    for g in greet:
        pl.semaphore_signal(barrier, inc=1, device_id=g, device_id_type=MESH)

    def rows(t):
        return pl.ds(t * CR, CR)

    loads = [pltpu.make_async_copy(frames.at[rows(t)], fr.at[rows(t)], fl_s.at[t]) for t in range(T)]
    for ld in loads:
        ld.start()

    def remote(src, dst, s, r, dev):
        return pltpu.make_async_remote_copy(
            src_ref=src, dst_ref=dst, send_sem=s, recv_sem=r, device_id=dev, device_id_type=MESH)

    def x_copy(t):
        return remote(a.at[rows(t)], ap.at[rows(t)], x_s.at[t], x_r.at[t], xdev(3))

    def dn_copy(t, src):
        return remote(src.at[rows(t)], nx.at[t, c], dn_s.at[t], dn_r.at[t], zdev(3))

    def up_copy(t, src):
        return remote(src.at[rows(t)], th.at[t, c], up_s.at[t], up_r.at[t], zdev(1))

    def ce_copy(t, src):
        return remote(src.at[rows(t)], ex.at[rows(t)], ce_s.at[t], ce_r.at[t], core)

    def cn_copy(t):
        return remote(nx.at[t, c], nx.at[t, c], cn_s.at[t], cn_r.at[t], core)

    def ct_copy(t):
        return remote(th.at[t, c], th.at[t, c], ct_s.at[t], ct_r.at[t], core)

    def cn_arrive(t):
        return remote(nx.at[t, 1 - c], nx.at[t, 1 - c], cn_s.at[t], cn_r.at[t], core)

    def ct_arrive(t):
        return remote(th.at[t, 1 - c], th.at[t, 1 - c], ct_s.at[t], ct_r.at[t], core)

    dk = dark[0:1, :]
    colsum = None
    for t in range(T):
        loads[t].wait()
        sig = fr[t * CR:(t + 1) * CR, :] - dk
        a[t * CR:(t + 1) * CR, :] = sig.astype(BF16)
        part = jnp.sum(sig, axis=0, keepdims=True)
        colsum = part if colsum is None else colsum + part
        if t == 0:
            pl.semaphore_wait(barrier, len(greet))
        x_copy(t).start()

        @pl.when(z >= 1)
        def _():
            dn_copy(t, a).start()

        @pl.when(z == 3)
        def _():
            up_copy(t, a).start()

        @pl.when(c == 1)
        def _():
            ce_copy(t, a).start()

    width = colsum.shape[1] // 8
    for i in range(8):
        cs[0, i:i + 1, :] = colsum[:, i * width:(i + 1) * width]

    def cs_copy(stage, i, dev):
        return remote(cs.at[stage], cr.at[i], cs_s.at[i], cs_r.at[i], dev)

    cs_copies = [cs_copy(0, 0, core)]
    cs_copies += [cs_copy(1, o, zdev(o)) for o in (1, 2, 3)]
    cs_copies += [cs_copy(2, 3 + o, xdev(o)) for o in (1, 2, 3)]
    cs_copies[0].start()
    cs_copies[0].wait_recv()
    cs[1] = cs[0] + cr[0]
    for i in (1, 2, 3):
        cs_copies[i].start()
    for i in (1, 2, 3):
        cs_copies[i].wait_recv()
    cs[2] = (cs[1] + cr[1]) + (cr[2] + cr[3])
    for i in (4, 5, 6):
        cs_copies[i].start()
    for i in (4, 5, 6):
        cs_copies[i].wait_recv()
    pixel_mean = ((cs[2] + cr[4]) + (cr[5] + cr[6])) / total_frames
    inv8 = 1.0 / pixel_mean
    for i in range(8):
        winv[0:1, i * width:(i + 1) * width] = inv8[i:i + 1, :]

    def arrive_ap(t):
        x_copy(t).wait_recv()

        @pl.when(z == 0)
        def _():
            dn_copy(t, ap).start()

        @pl.when(z <= 2)
        def _():
            up_copy(t, ap).start()

        @pl.when(c == 0)
        def _():
            ce_copy(t, ap).start()

    def arrive_nx(t):
        dn_copy(t, a).wait_recv()
        cn_copy(t).start()

    def arrive_th(t):
        up_copy(t, a).wait_recv()
        ct_copy(t).start()

    def y_copy(m, s0, ns, c0, nc, o):
        dst = lax.rem(y + o, 4)
        return remote(
            ys.at[pl.ds(s0, ns), :, pl.ds(pl.multiple_of(dst * 64, 64), 64), pl.ds(c0, nc)],
            yr.at[o - 1, pl.ds(s0, ns), :, :, pl.ds(c0, nc)],
            ys_s.at[m, o - 1], ys_r.at[m, o - 1], ydev(o))

    def z_copy(m, s0, ns, c0, nc):
        return remote(zs.at[pl.ds(s0, ns), :, pl.ds(c0, nc)], zr.at[pl.ds(s0, ns), :, pl.ds(c0, nc)],
                      zs_s.at[m], zs_r.at[m], zpartner)

    def sh_copy(m, c0, nc):
        return remote(shs.at[:, :, pl.ds(c0, nc)], shr.at[:, :, pl.ds(c0, nc)],
                      sh_s.at[m], sh_r.at[m], fwrap(2))

    messages = [(0, 0, 1, 0, BS), (1, 1, 1, 0, BS)]
    messages += [(2 + t, 2, 2, t * CR, CR) for t in range(T)]
    messages += [(2 + T + t, 4, 2, t * CR, CR) for t in range(T)]
    messages += [(2 + 2 * T + t, 6, 2, t * CR, CR) for t in range(T)]

    def y_start(m):
        for o in (2, 1, 3):
            y_copy(*messages[m], o).start()

    def z_start(m):
        _, s0, ns, c0, nc = messages[m]
        for o in (1, 2, 3):
            y_copy(*messages[m], o).wait_recv()
        mine = pl.ds(pl.multiple_of(y * 64, 64), 64)
        cols = pl.ds(c0, nc)

        def total(s, h):
            return (ys[s, h, mine, cols] + yr[0, s, h, :, cols]) + (yr[1, s, h, :, cols] + yr[2, s, h, :, cols])

        for s in range(s0, s0 + ns):
            zs[s, :, cols] = total(s, 1 - zl)
        z_copy(*messages[m]).start()
        for s in range(s0, s0 + ns):
            zo[s, :, cols] = total(s, zl)

    def z_end(m):
        _, s0, ns, c0, nc = messages[m]
        cols = pl.ds(c0, nc)
        z_copy(*messages[m]).wait_recv()
        for s in range(s0, s0 + ns):
            v = zo[s, :, cols] + zr[s, :, cols]
            if s0 == 6:
                shs[s - 6, :, cols] = v
            else:
                zo[s, :, cols] = v
        if s0 == 6:
            sh_copy(m - 2 - 2 * T, c0, nc).start()

    def pair_product(left, right, s0, t):
        for h in range(2):
            prod = nt_dot(left[h * 256:(h + 1) * 256, :], right[t].reshape(2 * CR, -1))
            ys[s0, h, :, t * CR:(t + 1) * CR] = prod[:, :CR]
            ys[s0 + 1, h, :, t * CR:(t + 1) * CR] = prod[:, CR:]

    def single_product(left, right, s0):
        for h in range(2):
            for q in range(2):
                ys[s0, h, :, q * 256:(q + 1) * 256] = nt_dot(
                    left[h * 256:(h + 1) * 256, :], right[q * 256:(q + 1) * 256, :])

    def step_nx(t):
        cn_arrive(t).wait_recv()
        pair_product(aw, nx, 2, t)
        y_start(2 + t)
        w = winv[0:1, :] * winv[0:1, :]
        nw[t * CR:(t + 1) * CR, :] = (nx[t, c].astype(F32) * w).astype(BF16)

    def step_th(t):
        ct_arrive(t).wait_recv()
        pair_product(aw, th, 4, t)
        y_start(2 + T + t)

    def step_nt(t):
        pair_product(nw, th, 6, t)
        y_start(2 + 2 * T + t)

    for t in range(T):
        w = winv[0:1, :] * winv[0:1, :]
        aw[t * CR:(t + 1) * CR, :] = ((fr[t * CR:(t + 1) * CR, :] - dk) * w).astype(BF16)
    inv = winv[0:1, :]
    hi = inv.astype(BF16).astype(F32)
    row = lax.broadcasted_iota(jnp.int32, (16, inv.shape[1]), 0)
    mix = jnp.where(row == 0, hi, jnp.where(row == 1, inv - hi, 0.0)).astype(BF16)
    fsum = jnp.sum(nt_dot(mix, a[...]), axis=0, keepdims=True)
    fs[0] = jnp.broadcast_to(fsum, (8, BS))

    def fy_copy(o):
        return remote(fs.at[0], fy.at[o - 1], fy_s.at[o - 1], fy_r.at[o - 1], ydev(o))

    fz_copy = remote(fs.at[1], fz, fz_s.at[0], fz_r.at[0], zpartner)

    def fm_copy(d):
        return remote(fmr.at[0], fmr.at[d], fm_s.at[d], fm_r.at[d], fwrap(-d))

    for o in (1, 2, 3):
        fy_copy(o).start()

    arrive_ap(0)
    single_product(aw, a, 0)
    y_start(0)

    for o in (1, 2, 3):
        fy_copy(o).wait_recv()
    fs[1] = (fs[0] + fy[0]) + (fy[1] + fy[2])
    fz_copy.start()
    fz_copy.wait_recv()
    fmr[0] = (fs[1] + fz[...]) / total_pix
    for d in range(1, BAND):
        fm_copy(d).start()

    arrive_ap(1)
    arrive_nx(0)
    arrive_ap(2)
    step_nx(0)
    arrive_th(0)
    z_start(0)
    arrive_ap(3)
    step_th(0)
    arrive_nx(1)
    for t in range(T):
        ce_copy(t, a).wait_recv()
    single_product(aw, ex, 1)
    y_start(1)
    z_end(0)
    z_start(2)
    step_nx(1)
    arrive_th(1)
    z_end(2)
    z_start(1)
    z_start(2 + T)
    step_th(1)
    arrive_nx(2)
    z_end(1)
    z_end(2 + T)
    z_start(3)
    step_nx(2)
    arrive_th(2)
    z_end(3)
    z_start(3 + T)
    step_th(2)
    arrive_nx(3)
    z_end(3 + T)
    z_start(4)
    z_start(4 + T)
    step_nx(3)
    for t in range(3):
        step_nt(t)
    z_end(4)
    z_end(4 + T)
    arrive_th(3)
    z_start(5)
    for t in range(3):
        z_start(2 + 2 * T + t)
    step_th(3)
    step_nt(3)
    z_end(5)
    for t in range(3):
        z_end(2 + 2 * T + t)
    z_start(5 + T)
    z_start(5 + 2 * T)
    z_end(5 + 2 * T)
    z_end(5 + T)

    for d in range(1, BAND):
        fm_copy(d).wait_recv()
    fcol[...] = jnp.transpose(jnp.broadcast_to(fmr[0, 0:1, :], (128, BS)))
    left = 1.0 / (fcol[pl.ds(pl.multiple_of(p * 64, 64), 64), :] * total_pix)
    left = jnp.concatenate([left] * (BS // 128), axis=1)
    for t in range(T):
        sh_copy(t, t * CR, CR).wait_recv()

    def finish(order):
        for lag in range(BAND):
            s = order[lag]
            v = shr[s - 6] if s >= 6 else zo[s]
            v = v * left * (1.0 / fmr[lag, 0:1, :])
            out[:, lag, :] = jnp.where(f + lag < nf, v, 0.0)

    @pl.when(c == 0)
    def _():
        finish((0, 1, 2, 3, 6, 7, 4, 5))

    @pl.when(c == 1)
    def _():
        finish((0, 2, 3, 6, 7, 4, 5, 1))

    for t in range(T):
        x_copy(t).wait_send()
        dn_copy(t, a).wait_send()
        up_copy(t, a).wait_send()
        ce_copy(t, a).wait_send()
        cn_copy(t).wait_send()
        ct_copy(t).wait_send()
        sh_copy(t, t * CR, CR).wait_send()
    for copy in cs_copies:
        copy.wait_send()
    for o in (1, 2, 3):
        fy_copy(o).wait_send()
    fz_copy.wait_send()
    for d in range(1, BAND):
        fm_copy(d).wait_send()
    for m in range(len(messages)):
        for o in (1, 2, 3):
            y_copy(*messages[m], o).wait_send()
        z_copy(*messages[m]).wait_send()


def on_device(frames, dark):
    n, pix = frames.shape
    total_frames = n * lax.axis_size("frame")
    total_pix = pix * lax.axis_size("pix")
    nm = 2 + 3 * T
    dma = pltpu.SemaphoreType.DMA
    vm = pltpu.VMEM
    out = pl.pallas_call(
        functools.partial(kernel, float(total_frames), float(total_pix)),
        out_shape=jax.ShapeDtypeStruct((64, BAND, BS), F32),
        in_specs=[pl.BlockSpec(memory_space=pl.ANY), pl.BlockSpec(memory_space=pltpu.VMEM)],
        out_specs=pl.BlockSpec(memory_space=pltpu.VMEM),
        scratch_shapes=[
            vm((BS, pix), F32), vm((BS, pix), BF16), vm((BS, pix), BF16), vm((BS, pix), BF16),
            vm((T, 2, CR, pix), BF16), vm((T, 2, CR, pix), BF16), vm((BS, pix), BF16), vm((BS, pix), BF16),
            vm((8, 2, 256, BS), F32), vm((3, 8, 2, 64, BS), F32),
            vm((8, 64, BS), F32), vm((8, 64, BS), F32), vm((8, 64, BS), F32),
            vm((2, 64, BS), F32), vm((2, 64, BS), F32),
            vm((3, 8, pix // 8), F32), vm((7, 8, pix // 8), F32), vm((8, pix), F32),
            vm((2, 8, BS), F32), vm((3, 8, BS), F32), vm((8, BS), F32), vm((BAND, 8, BS), F32), vm((BS, 128), F32),
            dma((T,)),
            dma((T,)), dma((T,)), dma((T,)), dma((T,)), dma((T,)), dma((T,)),
            dma((T,)), dma((T,)), dma((T,)), dma((T,)), dma((T,)), dma((T,)),
            dma((nm, 3)), dma((nm, 3)), dma((nm,)), dma((nm,)), dma((T,)), dma((T,)),
            dma((7,)), dma((7,)), dma((3,)), dma((3,)), dma((1,)), dma((1,)), dma((BAND,)), dma((BAND,)),
        ],
        compiler_params=pltpu.CompilerParams(
            collective_id=0, has_side_effects=True, vmem_limit_bytes=56 * 1024 * 1024),
        cost_estimate=pl.CostEstimate(flops=2 * 8 * BS * BS * pix, bytes_accessed=6 * BS * pix, transcendentals=0),
    )(frames, dark.reshape(1, pix))
    return out.reshape(64, 1, BAND, BS)


def solution(mesh):
    return jax.shard_map(
        on_device,
        mesh=mesh,
        in_specs=(P("frame", "pix"), P("pix")),
        out_specs=P("pix", "frame", None, None),
        check_vma=False,
    )
```

```python
import functools

import jax
import jax.numpy as jnp
from jax import lax
from jax.experimental import pallas as pl
from jax.experimental.pallas import tpu as pltpu
from jax.sharding import PartitionSpec as P

BS = 512
SH = 64
T = 4
CS = SH // T
CR = BS // T
BAND = 8
F32 = jnp.float32
BF16 = jnp.bfloat16
MESH = pl.DeviceIdType.MESH


def nt_dot(left, right):
    return lax.dot_general(left, right, (((1,), (1,)), ((), ())), preferred_element_type=F32)


def natural(v):
    lane = lax.broadcasted_iota(jnp.int32, (v.shape[0], CR), 1)
    groups = []
    for g in range(BS // CR):
        acc = None
        for t in range(T):
            src = v[:, t * CR:(t + 1) * CR]
            for h in range(2):
                shift = (h * SH + t * CS) - (2 * g + h) * CS
                piece = pltpu.roll(src, shift % CR, 1) if shift % CR else src
                if acc is None:
                    acc = piece
                else:
                    start = h * SH + t * CS
                    acc = jnp.where((lane >= start) & (lane < start + CS), piece, acc)
        groups.append(acc)
    return jnp.concatenate(groups, axis=1)


def kernel(total_frames, total_pix, frames, dark, out,
           fr, a, aw, ap, ex, rv, nw, lw, ys, yr, zs, zo, zr, hs, hb,
           cs, cr, winv, fs, fy, fz, fmr, fcol,
           fl_s, x_s, x_r, e_s, e_r, l_s, l_r, ce_s, ce_r, c_s, c_r,
           ys_s, ys_r, zs_s, zs_r, hs_s, hb_r, cs_s, cs_r, fy_s, fy_r, fz_s, fz_r, fm_s, fm_r):
    f = lax.axis_index("frame")
    p = lax.axis_index("pix")
    nf = 32
    pix = fr.shape[1]
    c = lax.rem(f, 2)
    k = f // 2
    z = lax.rem(k, 4)
    x = k // 4
    y = lax.rem(p, 4)
    zl = p // 4

    def fdev(nx_, nz_, nc_):
        return ((nx_ * 4 + nz_) * 2 + nc_, p)

    def kdev(d):
        return (lax.rem(k + d, 16) * 2 + c, p)

    def fwrap(d):
        return (lax.rem(f + d + nf, nf), p)

    def zdev(o):
        return fdev(x, lax.rem(z + o, 4), c)

    def xdev(o):
        return fdev(lax.rem(x + o, 4), z, c)

    def ydev(o):
        return (f, zl * 4 + lax.rem(y + o, 4))

    core = fdev(x, z, 1 - c)
    zpartner = (f, (1 - zl) * 4 + y)
    plane = [core] + [fdev(x, lax.rem(z + o, 4), cc) for o in (1, 2, 3) for cc in (c, 1 - c)]
    homes = [(lax.rem(f + 2, nf), h * 4 + y) for h in range(2)]

    barrier = pltpu.get_barrier_semaphore()
    greet = [zpartner] + plane
    greet += [xdev(o) for o in (1, 2, 3)]
    greet += [ydev(o) for o in (1, 2, 3)]
    greet += [fwrap(d) for d in range(1, 8)]
    greet += [(lax.rem(f + nf - 2, nf), h * 4 + y) for h in range(2)]
    greet += [kdev(3 - 2 * zl), kdev(1 + 2 * zl)]
    for g in greet:
        pl.semaphore_signal(barrier, inc=1, device_id=g, device_id_type=MESH)

    rows = BS // 4
    loads = [pltpu.make_async_copy(frames.at[pl.ds(q * rows, rows)], fr.at[pl.ds(q * rows, rows)], fl_s.at[q])
             for q in range(4)]
    for ld in loads:
        ld.start()

    def remote(src, dst, s, r, dev):
        return pltpu.make_async_remote_copy(
            src_ref=src, dst_ref=dst, send_sem=s, recv_sem=r, device_id=dev, device_id_type=MESH)

    def part(ref, t):
        return ref.at[:, pl.ds(t * CS, CS), :]

    def x_copy(t):
        return remote(part(a, t), part(ap, t), x_s.at[t], x_r.at[t], xdev(3))

    def e_copy(t):
        return remote(part(a, t), rv.at[0, t, c], e_s.at[t], e_r.at[t], kdev(13 + 2 * zl))

    def l_copy(t, src, dev):
        return remote(part(src, t), rv.at[1, t, c], l_s.at[t], l_r.at[t], dev)

    def ce_copy(t, src):
        return remote(part(src, t), part(ex, t), ce_s.at[t], ce_r.at[t], core)

    def c_copy(e, t):
        return remote(rv.at[e, t, c], rv.at[e, t, c], c_s.at[e, t], c_r.at[e, t], core)

    dk = dark[0:1, :]
    colsum = None
    for q in range(4):
        loads[q].wait()
        sig = fr[q * rows:(q + 1) * rows, :] - dk
        a[2 * q:2 * q + 2] = sig.astype(BF16).reshape(2, SH, pix)
        partial = jnp.sum(sig, axis=0, keepdims=True)
        colsum = partial if colsum is None else colsum + partial

    width = pix // 8
    for i in range(8):
        cs[0, i:i + 1, :] = colsum[:, i * width:(i + 1) * width]

    def cs_copy(stage, i, dev):
        return remote(cs.at[stage], cr.at[i], cs_s.at[i], cs_r.at[i], dev)

    pl.semaphore_wait(barrier, len(greet))
    cs_copies = [cs_copy(0, i, d) for i, d in enumerate(plane)]
    cs_copies += [cs_copy(1, 6 + o, xdev(o)) for o in (1, 2, 3)]
    for copy in cs_copies[:7]:
        copy.start()
    along = z >= 3 - 2 * zl

    @pl.when(along)
    def _():
        for t in range(T):
            e_copy(t).start()

    for copy in cs_copies[:7]:
        copy.wait_recv()
    cs[1] = ((cs[0] + cr[0]) + (cr[1] + cr[2])) + ((cr[3] + cr[4]) + (cr[5] + cr[6]))
    for copy in cs_copies[7:]:
        copy.start()

    @pl.when(jnp.logical_not(along))
    def _():
        for t in range(2):
            e_copy(t).start()

    @pl.when(c == 0)
    def _():
        x_copy(0).start()

    @pl.when(jnp.logical_not(along))
    def _():
        for t in range(2, T):
            e_copy(t).start()

    @pl.when(c == 0)
    def _():
        for t in range(1, T):
            x_copy(t).start()

    @pl.when(c == 1)
    def _():
        for t in range(T):
            ce_copy(t, a).start()

    for copy in cs_copies[7:]:
        copy.wait_recv()
    pixel_mean = ((cs[1] + cr[7]) + (cr[8] + cr[9])) / total_frames
    inv8 = 1.0 / pixel_mean
    for i in range(8):
        winv[0:1, i * width:(i + 1) * width] = inv8[i:i + 1, :]

    def scaled(v):
        w = winv[0:1, :] * winv[0:1, :]
        return (v.astype(F32) * w).astype(BF16)

    early = 4 - 2 * zl
    late = 2 + 2 * zl
    m_self, m_ex, m_early, m_late, m_far = 0, 1, 2, 2 + T, 2 + 2 * T
    messages = [(0, 0, 1, 0, BS), (1, 1, 1, 0, BS)]
    messages += [(m_early + t, early, 2, t * CR, CR) for t in range(T)]
    messages += [(m_late + t, late, 2, t * CR, CR) for t in range(T)]

    def y_copy(m, o):
        dst = lax.rem(y + o, 4)
        _, s0, ns, c0, nc = messages[m]
        return remote(
            ys.at[pl.ds(s0, ns), :, dst, :, pl.ds(c0, nc)], yr.at[o - 1, pl.ds(s0, ns), :, :, pl.ds(c0, nc)],
            ys_s.at[m, o - 1], ys_r.at[m, o - 1], ydev(o))

    def far_rows(t, o):
        dst = lax.rem(y + o, 4)
        return remote(
            ys.at[pl.ds(6, 2), :, dst, pl.ds(t * CS, CS), :], yr.at[o - 1, pl.ds(6, 2), :, pl.ds(t * CS, CS), :],
            ys_s.at[m_far + t, o - 1], ys_r.at[m_far + t, o - 1], ydev(o))

    def far_cols(t, o):
        dst = lax.rem(y + o, 4)
        return remote(
            ys.at[pl.ds(6, 2), :, dst, :, pl.ds(t * CR, CR)], yr.at[o - 1, pl.ds(6, 2), :, :, pl.ds(t * CR, CR)],
            ys_s.at[m_far + t, o - 1], ys_r.at[m_far + t, o - 1], ydev(o))

    def y_start(m):
        for o in (2, 1, 3):
            y_copy(m, o).start()

    def z_copy(m):
        _, s0, ns, c0, nc = messages[m]
        return remote(zs.at[pl.ds(s0, ns), :, pl.ds(c0, nc)], zr.at[pl.ds(s0, ns), :, pl.ds(c0, nc)],
                      zs_s.at[m], zs_r.at[m], zpartner)

    def total(s, h, r, q):
        return (ys[s, h, y, r, q] + yr[0, s, h, r, q]) + (yr[1, s, h, r, q] + yr[2, s, h, r, q])

    def z_start(m):
        _, s0, ns, c0, nc = messages[m]
        for o in (1, 2, 3):
            y_copy(m, o).wait_recv()
        cols = pl.ds(c0, nc)
        for i in range(ns):
            zs[s0 + i, :, cols] = total(s0 + i, 1 - zl, slice(None), cols)
        z_copy(m).start()
        for i in range(ns):
            zo[s0 + i, :, cols] = total(s0 + i, zl, slice(None), cols)

    def home_copy(t, h, r, q):
        return remote(hs.at[h, :, r, q], hb.at[zl, :, r, q], hs_s.at[t, h], hb_r.at[zl, t], homes[h])

    def far_home(t):
        @pl.when(zl == 0)
        def _():
            r, q = pl.ds(t * CS, CS), pl.ds(0, BS)
            for o in (1, 2, 3):
                far_rows(t, o).wait_recv()
            for h in range(2):
                for j in range(2):
                    hs[h, j, r, :] = total(6 + j, h, r, q)
                home_copy(t, h, r, q).start()

        @pl.when(zl == 1)
        def _():
            r, q = pl.ds(0, SH), pl.ds(t * CR, CR)
            for o in (1, 2, 3):
                far_cols(t, o).wait_recv()
            for h in range(2):
                for j in range(2):
                    hs[h, j, :, q] = total(6 + j, h, r, q)
                home_copy(t, h, r, q).start()

    def pair_product(left, e, s0, t):
        right = rv[e, t].reshape(2 * CR, pix)
        for h in range(2):
            prod = nt_dot(left[4 * h:4 * h + 4].reshape(4 * SH, pix), right)
            for j in range(2):
                ys[s0 + j, h, :, :, t * CR:(t + 1) * CR] = prod[:, j * CR:(j + 1) * CR].reshape(4, SH, CR)

    def single_product(left, right, s):
        for h in range(2):
            for q in range(2):
                prod = nt_dot(left[4 * h:4 * h + 4].reshape(4 * SH, pix), right[4 * q:4 * q + 4].reshape(4 * SH, pix))
                ys[s, h, :, :, q * 256:(q + 1) * 256] = prod.reshape(4, SH, 256)

    def far_product(t):
        @pl.when(zl == 0)
        def _():
            lw[...] = scaled(rv[1, t, c].reshape(CR, pix))
            for q in range(T):
                prod = nt_dot(lw[...], rv[0, q].reshape(2 * CR, pix))
                for j in range(2):
                    ys[6 + j, :, :, t * CS:(t + 1) * CS, q * CR:(q + 1) * CR] = (
                        prod[:, j * CR:(j + 1) * CR].reshape(2, 4, CS, CR))
            for o in (2, 1, 3):
                far_rows(t, o).start()

        @pl.when(zl == 1)
        def _():
            pair_product(nw, 1, 6, t)
            for o in (2, 1, 3):
                far_cols(t, o).start()

    def arrive_early(t):
        e_copy(t).wait_recv()
        c_copy(0, t).start()

    def step_early(t):
        c_copy(0, t).wait_recv()
        pair_product(aw, 0, early, t)
        y_start(m_early + t)

        @pl.when(zl == 1)
        def _():
            nw[:, t * CS:(t + 1) * CS, :] = scaled(rv[0, t, c])

    forward = (c == 0) & (z <= 2 * zl)

    def send_late(t):
        @pl.when(forward)
        def _():
            x_copy(t).wait_recv()
            l_copy(t, ap, zdev(3 - 2 * zl)).start()

        @pl.when(jnp.logical_not(forward))
        def _():
            l_copy(t, a, kdev(15 - 2 * zl)).start()

    def send_extra(t):
        @pl.when(c == 0)
        def _():
            @pl.when(jnp.logical_not(forward))
            def _():
                x_copy(t).wait_recv()

            ce_copy(t, ap).start()

    def arrive_late(t):
        l_copy(t, a, core).wait_recv()
        c_copy(1, t).start()

    def step_late(t):
        c_copy(1, t).wait_recv()
        pair_product(aw, 1, late, t)
        y_start(m_late + t)
        far_product(t)

    for q in range(4):
        aw[2 * q:2 * q + 2] = scaled(fr[q * rows:(q + 1) * rows, :] - dk).reshape(2, SH, pix)
    inv = winv[0:1, :]
    hi = inv.astype(BF16).astype(F32)
    row = lax.broadcasted_iota(jnp.int32, (16, pix), 0)
    mix = jnp.where(row == 0, hi, jnp.where(row == 1, inv - hi, 0.0)).astype(BF16)
    fsum = jnp.sum(nt_dot(mix, a[...].reshape(BS, pix)), axis=0, keepdims=True)
    fs[0] = jnp.broadcast_to(fsum, (8, BS))

    def fy_copy(o):
        return remote(fs.at[0], fy.at[o - 1], fy_s.at[o - 1], fy_r.at[o - 1], ydev(o))

    fz_copy = remote(fs.at[1], fz, fz_s.at[0], fz_r.at[0], zpartner)

    def fm_copy(d):
        return remote(fmr.at[0], fmr.at[d], fm_s.at[d], fm_r.at[d], fwrap(-d))

    for o in (1, 2, 3):
        fy_copy(o).start()
    single_product(aw, a, 0)
    y_start(m_self)
    for o in (1, 2, 3):
        fy_copy(o).wait_recv()
    fs[1] = (fs[0] + fy[0]) + (fy[1] + fy[2])
    fz_copy.start()

    arrive_early(0)
    step_early(0)
    arrive_early(1)
    z_start(m_self)
    step_early(1)
    arrive_early(2)
    send_late(0)
    z_start(m_early)
    step_early(2)
    send_late(1)
    arrive_early(3)
    send_late(2)
    send_late(3)
    z_start(m_early + 1)
    step_early(3)
    for t in range(T):
        send_extra(t)
    fz_copy.wait_recv()
    fmr[0] = (fs[1] + fz[...]) / total_pix
    for d in range(1, BAND):
        fm_copy(d).start()
    for t in range(T):
        ce_copy(t, a).wait_recv()
    single_product(aw, ex, 1)
    y_start(m_ex)
    z_start(m_early + 2)
    arrive_late(0)
    z_start(m_early + 3)
    step_late(0)
    z_start(m_ex)
    arrive_late(1)
    z_start(m_late)
    step_late(1)
    far_home(0)
    arrive_late(2)
    z_start(m_late + 1)
    step_late(2)
    far_home(1)

    for d in range(1, BAND):
        fm_copy(d).wait_recv()
    fcol[...] = jnp.transpose(jnp.broadcast_to(fmr[0, 0:1, :], (128, BS)))
    left = 1.0 / (fcol[pl.ds(pl.multiple_of(p * SH, SH), SH), :] * total_pix)
    left = jnp.concatenate([left] * (BS // 128), axis=1)

    def put(lag, v):
        v = v * left * (1.0 / fmr[lag, 0:1, :])
        out[:, lag, :] = jnp.where(f + lag < nf, v, 0.0)

    z_copy(m_self).wait_recv()
    put(0, zo[0] + zr[0])
    z_copy(m_ex).wait_recv()

    @pl.when(c == 0)
    def _():
        put(1, zo[1] + zr[1])

    @pl.when(c == 1)
    def _():
        put(7, zo[1] + zr[1])

    arrive_late(3)
    z_start(m_late + 2)
    step_late(3)
    far_home(2)
    z_start(m_late + 3)
    far_home(3)
    for t in range(T):
        z_copy(m_early + t).wait_recv()
        z_copy(m_late + t).wait_recv()

    def put_pairs(base):
        for j in range(2):
            put(base[0] + j, natural(zo[2 + j] + zr[2 + j]))
            put(base[1] + j, natural(zo[4 + j] + zr[4 + j]))

    @pl.when(c == 0)
    def _():
        put_pairs((2, 6))

    @pl.when(c == 1)
    def _():
        put_pairs((1, 5))

    for t in range(T):
        for w in range(2):
            remote(hs.at[0, :, :, pl.ds(0, CR)], hb.at[w, :, :, pl.ds(0, CR)], hs_s.at[t, 0], hb_r.at[w, t],
                   homes[0]).wait_recv()

    def put_far(base):
        for j in range(2):
            put(base + j, natural(hb[0, j] + hb[1, j]))

    @pl.when(c == 0)
    def _():
        put_far(4)

    @pl.when(c == 1)
    def _():
        put_far(3)

    @pl.when(c == 0)
    def _():
        for t in range(T):
            x_copy(t).wait_send()

    for t in range(T):
        e_copy(t).wait_send()
        l_copy(t, a, core).wait_send()
        ce_copy(t, a).wait_send()
        for e in range(2):
            c_copy(e, t).wait_send()
        for h in range(2):
            home_copy(t, h, pl.ds(0, SH), pl.ds(0, CR)).wait_send()
        for o in (1, 2, 3):
            far_cols(t, o).wait_send()
    for copy in cs_copies:
        copy.wait_send()
    for o in (1, 2, 3):
        fy_copy(o).wait_send()
    fz_copy.wait_send()
    for d in range(1, BAND):
        fm_copy(d).wait_send()
    for m in range(len(messages)):
        for o in (1, 2, 3):
            y_copy(m, o).wait_send()
        z_copy(m).wait_send()


def on_device(frames, dark):
    n, pix = frames.shape
    total_frames = n * lax.axis_size("frame")
    total_pix = pix * lax.axis_size("pix")
    nm = 2 + 3 * T
    nz = 2 + 2 * T
    dma = pltpu.SemaphoreType.DMA
    vm = pltpu.VMEM
    block = (8, SH, pix)
    out = pl.pallas_call(
        functools.partial(kernel, float(total_frames), float(total_pix)),
        out_shape=jax.ShapeDtypeStruct((SH, BAND, BS), F32),
        in_specs=[pl.BlockSpec(memory_space=pl.ANY), pl.BlockSpec(memory_space=pltpu.VMEM)],
        out_specs=pl.BlockSpec(memory_space=pltpu.VMEM),
        scratch_shapes=[
            vm((BS, pix), F32), vm(block, BF16), vm(block, BF16), vm(block, BF16), vm(block, BF16),
            vm((2, T, 2, 8, CS, pix), BF16), vm(block, BF16), vm((CR, pix), BF16),
            vm((8, 2, 4, SH, BS), F32), vm((3, 8, 2, SH, BS), F32),
            vm((6, SH, BS), F32), vm((6, SH, BS), F32), vm((6, SH, BS), F32),
            vm((2, 2, SH, BS), F32), vm((2, 2, SH, BS), F32),
            vm((2, 8, pix // 8), F32), vm((10, 8, pix // 8), F32), vm((8, pix), F32),
            vm((2, 8, BS), F32), vm((3, 8, BS), F32), vm((8, BS), F32), vm((BAND, 8, BS), F32), vm((BS, 128), F32),
            dma((4,)),
            dma((T,)), dma((T,)), dma((T,)), dma((T,)), dma((T,)), dma((T,)),
            dma((T,)), dma((T,)), dma((2, T)), dma((2, T)),
            dma((nm, 3)), dma((nm, 3)), dma((nz,)), dma((nz,)), dma((T, 2)), dma((2, T)),
            dma((10,)), dma((10,)), dma((3,)), dma((3,)), dma((1,)), dma((1,)), dma((BAND,)), dma((BAND,)),
        ],
        compiler_params=pltpu.CompilerParams(
            collective_id=0, has_side_effects=True, vmem_limit_bytes=56 * 1024 * 1024),
        cost_estimate=pl.CostEstimate(flops=2 * 8 * BS * BS * pix, bytes_accessed=6 * BS * pix, transcendentals=0),
    )(frames, dark.reshape(1, pix))
    return out.reshape(SH, 1, BAND, BS)


def solution(mesh):
    return jax.shard_map(
        on_device,
        mesh=mesh,
        in_specs=(P("frame", "pix"), P("pix")),
        out_specs=P("pix", "frame", None, None),
        check_vma=False,
    )
```

```python
import functools

import jax
import jax.numpy as jnp
from jax import lax
from jax.experimental import pallas as pl
from jax.experimental.pallas import tpu as pltpu
from jax.sharding import PartitionSpec as P

BS = 512
SH = 64
T = 4
CS = SH // T
CR = BS // T
BAND = 8
F32 = jnp.float32
BF16 = jnp.bfloat16
MESH = pl.DeviceIdType.MESH


def nt_dot(left, right):
    return lax.dot_general(left, right, (((1,), (1,)), ((), ())), preferred_element_type=F32)


def natural(v):
    lane = lax.broadcasted_iota(jnp.int32, (v.shape[0], CR), 1)
    groups = []
    for g in range(BS // CR):
        acc = None
        for t in range(T):
            src = v[:, t * CR:(t + 1) * CR]
            for h in range(2):
                shift = (h * SH + t * CS) - (2 * g + h) * CS
                piece = pltpu.roll(src, shift % CR, 1) if shift % CR else src
                if acc is None:
                    acc = piece
                else:
                    start = h * SH + t * CS
                    acc = jnp.where((lane >= start) & (lane < start + CS), piece, acc)
        groups.append(acc)
    return jnp.concatenate(groups, axis=1)


def kernel(total_frames, total_pix, frames, dark, out,
           fr, a, aw, ap, ex, rv, nw, lw, ys, yr, zs, zo, zr, hs, hb,
           cs, cr, winv, fs, fy, fz, fmr, fcol,
           fl_s, x_s, x_r, e_s, e_r, l_s, l_r, ce_s, ce_r, c_s, c_r,
           ys_s, ys_r, zs_s, zs_r, hs_s, hb_r, cs_s, cs_r, fy_s, fy_r, fz_s, fz_r, fm_s, fm_r):
    f = lax.axis_index("frame")
    p = lax.axis_index("pix")
    nf = 32
    pix = fr.shape[1]
    c = lax.rem(f, 2)
    k = f // 2
    z = lax.rem(k, 4)
    x = k // 4
    y = lax.rem(p, 4)
    zl = p // 4

    def fdev(nx_, nz_, nc_):
        return ((nx_ * 4 + nz_) * 2 + nc_, p)

    def kdev(d):
        return (lax.rem(k + d, 16) * 2 + c, p)

    def fwrap(d):
        return (lax.rem(f + d + nf, nf), p)

    def zdev(o):
        return fdev(x, lax.rem(z + o, 4), c)

    def xdev(o):
        return fdev(lax.rem(x + o, 4), z, c)

    def ydev(o):
        return (f, zl * 4 + lax.rem(y + o, 4))

    core = fdev(x, z, 1 - c)
    zpartner = (f, (1 - zl) * 4 + y)
    plane = [core] + [fdev(x, lax.rem(z + o, 4), cc) for o in (1, 2, 3) for cc in (c, 1 - c)]
    homes = [(lax.rem(f + 2, nf), h * 4 + y) for h in range(2)]

    barrier = pltpu.get_barrier_semaphore()
    greet = [zpartner] + plane
    greet += [xdev(o) for o in (1, 2, 3)]
    greet += [ydev(o) for o in (1, 2, 3)]
    greet += [fwrap(d) for d in range(1, 8)]
    greet += [(lax.rem(f + nf - 2, nf), h * 4 + y) for h in range(2)]
    greet += [kdev(3 - 2 * zl), kdev(1 + 2 * zl)]
    for g in greet:
        pl.semaphore_signal(barrier, inc=1, device_id=g, device_id_type=MESH)

    rows = BS // 4
    loads = [pltpu.make_async_copy(frames.at[pl.ds(q * rows, rows)], fr.at[pl.ds(q * rows, rows)], fl_s.at[q])
             for q in range(4)]
    for ld in loads:
        ld.start()

    def remote(src, dst, s, r, dev):
        return pltpu.make_async_remote_copy(
            src_ref=src, dst_ref=dst, send_sem=s, recv_sem=r, device_id=dev, device_id_type=MESH)

    def part(ref, t):
        return ref.at[:, pl.ds(t * CS, CS), :]

    def x_copy(t):
        return remote(part(a, t), part(ap, t), x_s.at[t], x_r.at[t], xdev(3))

    def e_copy(t):
        return remote(part(a, t), rv.at[0, t, c], e_s.at[t], e_r.at[t], kdev(13 + 2 * zl))

    def l_copy(t, src, dev):
        return remote(part(src, t), rv.at[1, t, c], l_s.at[t], l_r.at[t], dev)

    def ce_copy(t, src):
        return remote(part(src, t), part(ex, t), ce_s.at[t], ce_r.at[t], core)

    def c_copy(e, t):
        return remote(rv.at[e, t, c], rv.at[e, t, c], c_s.at[e, t], c_r.at[e, t], core)

    dk = dark[0:1, :]
    colsum = None
    for q in range(4):
        loads[q].wait()
        sig = fr[q * rows:(q + 1) * rows, :] - dk
        a[2 * q:2 * q + 2] = sig.astype(BF16).reshape(2, SH, pix)
        partial = jnp.sum(sig, axis=0, keepdims=True)
        colsum = partial if colsum is None else colsum + partial

    width = pix // 8
    for i in range(8):
        cs[0, i:i + 1, :] = colsum[:, i * width:(i + 1) * width]

    def cs_copy(stage, i, dev):
        return remote(cs.at[stage], cr.at[i], cs_s.at[i], cs_r.at[i], dev)

    pl.semaphore_wait(barrier, len(greet))
    cs_copies = [cs_copy(0, i, d) for i, d in enumerate(plane)]
    cs_copies += [cs_copy(1, 6 + o, xdev(o)) for o in (1, 2, 3)]
    for copy in cs_copies[:7]:
        copy.start()
    along = z >= 3 - 2 * zl

    @pl.when(along)
    def _():
        for t in range(T):
            e_copy(t).start()

    for copy in cs_copies[:7]:
        copy.wait_recv()
    cs[1] = ((cs[0] + cr[0]) + (cr[1] + cr[2])) + ((cr[3] + cr[4]) + (cr[5] + cr[6]))
    for copy in cs_copies[7:]:
        copy.start()

    for t in range(T):
        @pl.when(jnp.logical_not(along))
        def _():
            e_copy(t).start()

        @pl.when(c == 0)
        def _():
            x_copy(t).start()

    @pl.when(c == 1)
    def _():
        for t in range(T):
            ce_copy(t, a).start()

    for copy in cs_copies[7:]:
        copy.wait_recv()
    pixel_mean = ((cs[1] + cr[7]) + (cr[8] + cr[9])) / total_frames
    inv8 = 1.0 / pixel_mean
    for i in range(8):
        winv[0:1, i * width:(i + 1) * width] = inv8[i:i + 1, :]

    def scaled(v):
        w = winv[0:1, :] * winv[0:1, :]
        return (v.astype(F32) * w).astype(BF16)

    early = 4 - 2 * zl
    late = 2 + 2 * zl
    m_self, m_ex, m_early, m_late, m_far = 0, 1, 2, 2 + T, 2 + 2 * T
    messages = [(0, 0, 1, 0, BS), (1, 1, 1, 0, BS)]
    messages += [(m_early + t, early, 2, t * CR, CR) for t in range(T)]
    messages += [(m_late + t, late, 2, t * CR, CR) for t in range(T)]

    def y_copy(m, o):
        dst = lax.rem(y + o, 4)
        _, s0, ns, c0, nc = messages[m]
        return remote(
            ys.at[pl.ds(s0, ns), :, dst, :, pl.ds(c0, nc)], yr.at[o - 1, pl.ds(s0, ns), :, :, pl.ds(c0, nc)],
            ys_s.at[m, o - 1], ys_r.at[m, o - 1], ydev(o))

    def far_rows(t, o):
        dst = lax.rem(y + o, 4)
        return remote(
            ys.at[pl.ds(6, 2), :, dst, pl.ds(t * CS, CS), :], yr.at[o - 1, pl.ds(6, 2), :, pl.ds(t * CS, CS), :],
            ys_s.at[m_far + t, o - 1], ys_r.at[m_far + t, o - 1], ydev(o))

    def far_cols(t, o):
        dst = lax.rem(y + o, 4)
        return remote(
            ys.at[pl.ds(6, 2), :, dst, :, pl.ds(t * CR, CR)], yr.at[o - 1, pl.ds(6, 2), :, :, pl.ds(t * CR, CR)],
            ys_s.at[m_far + t, o - 1], ys_r.at[m_far + t, o - 1], ydev(o))

    def y_start(m):
        for o in (2, 1, 3):
            y_copy(m, o).start()

    def z_copy(m):
        _, s0, ns, c0, nc = messages[m]
        return remote(zs.at[pl.ds(s0, ns), :, pl.ds(c0, nc)], zr.at[pl.ds(s0, ns), :, pl.ds(c0, nc)],
                      zs_s.at[m], zs_r.at[m], zpartner)

    def total(s, h, r, q):
        return (ys[s, h, y, r, q] + yr[0, s, h, r, q]) + (yr[1, s, h, r, q] + yr[2, s, h, r, q])

    def z_sum(m):
        _, s0, ns, c0, nc = messages[m]
        for o in (1, 2, 3):
            y_copy(m, o).wait_recv()
        cols = pl.ds(c0, nc)
        for i in range(ns):
            zs[s0 + i, :, cols] = total(s0 + i, 1 - zl, slice(None), cols)
        for i in range(ns):
            zo[s0 + i, :, cols] = total(s0 + i, zl, slice(None), cols)

    def z_start(m):
        z_sum(m)
        z_copy(m).start()

    def home_copy(t, h, r, q):
        return remote(hs.at[h, :, r, q], hb.at[zl, :, r, q], hs_s.at[t, h], hb_r.at[zl, t], homes[h])

    def far_sum(t):
        @pl.when(zl == 0)
        def _():
            r, q = pl.ds(t * CS, CS), pl.ds(0, BS)
            for o in (1, 2, 3):
                far_rows(t, o).wait_recv()
            for h in range(2):
                for j in range(2):
                    hs[h, j, r, :] = total(6 + j, h, r, q)

        @pl.when(zl == 1)
        def _():
            r, q = pl.ds(0, SH), pl.ds(t * CR, CR)
            for o in (1, 2, 3):
                far_cols(t, o).wait_recv()
            for h in range(2):
                for j in range(2):
                    hs[h, j, :, q] = total(6 + j, h, r, q)

    def far_send(t):
        @pl.when(zl == 0)
        def _():
            for h in range(2):
                home_copy(t, h, pl.ds(t * CS, CS), pl.ds(0, BS)).start()

        @pl.when(zl == 1)
        def _():
            for h in range(2):
                home_copy(t, h, pl.ds(0, SH), pl.ds(t * CR, CR)).start()

    def far_home(t):
        far_sum(t)
        far_send(t)

    def pair_product(left, e, s0, t):
        right = rv[e, t].reshape(2 * CR, pix)
        for h in range(2):
            prod = nt_dot(left[4 * h:4 * h + 4].reshape(4 * SH, pix), right)
            for j in range(2):
                ys[s0 + j, h, :, :, t * CR:(t + 1) * CR] = prod[:, j * CR:(j + 1) * CR].reshape(4, SH, CR)

    def single_product(left, right, s):
        for h in range(2):
            for q in range(2):
                prod = nt_dot(left[4 * h:4 * h + 4].reshape(4 * SH, pix), right[4 * q:4 * q + 4].reshape(4 * SH, pix))
                ys[s, h, :, :, q * 256:(q + 1) * 256] = prod.reshape(4, SH, 256)

    def far_product(t):
        @pl.when(zl == 0)
        def _():
            lw[...] = scaled(rv[1, t, c].reshape(CR, pix))
            for q in range(T):
                prod = nt_dot(lw[...], rv[0, q].reshape(2 * CR, pix))
                for j in range(2):
                    ys[6 + j, :, :, t * CS:(t + 1) * CS, q * CR:(q + 1) * CR] = (
                        prod[:, j * CR:(j + 1) * CR].reshape(2, 4, CS, CR))
            for o in (2, 1, 3):
                far_rows(t, o).start()

        @pl.when(zl == 1)
        def _():
            pair_product(nw, 1, 6, t)
            for o in (2, 1, 3):
                far_cols(t, o).start()

    def arrive_early(t):
        e_copy(t).wait_recv()
        c_copy(0, t).start()

    def step_early(t):
        c_copy(0, t).wait_recv()
        pair_product(aw, 0, early, t)
        y_start(m_early + t)

        @pl.when(zl == 1)
        def _():
            nw[:, t * CS:(t + 1) * CS, :] = scaled(rv[0, t, c])

    forward = (c == 0) & (z <= 2 * zl)

    def send_late():
        @pl.when(jnp.logical_not(forward))
        def _():
            for t in range(T):
                l_copy(t, a, kdev(15 - 2 * zl)).start()

    def forward_late(t):
        @pl.when(forward)
        def _():
            x_copy(t).wait_recv()
            l_copy(t, ap, zdev(3 - 2 * zl)).start()

    def send_extra(t):
        @pl.when(c == 0)
        def _():
            @pl.when(jnp.logical_not(forward))
            def _():
                x_copy(t).wait_recv()

            ce_copy(t, ap).start()

    def arrive_late(t):
        l_copy(t, a, core).wait_recv()
        c_copy(1, t).start()

    def step_late(t):
        c_copy(1, t).wait_recv()
        pair_product(aw, 1, late, t)
        y_start(m_late + t)
        far_product(t)

    for q in range(4):
        aw[2 * q:2 * q + 2] = scaled(fr[q * rows:(q + 1) * rows, :] - dk).reshape(2, SH, pix)
    inv = winv[0:1, :]
    hi = inv.astype(BF16).astype(F32)
    row = lax.broadcasted_iota(jnp.int32, (16, pix), 0)
    mix = jnp.where(row == 0, hi, jnp.where(row == 1, inv - hi, 0.0)).astype(BF16)
    fsum = jnp.sum(nt_dot(mix, a[...].reshape(BS, pix)), axis=0, keepdims=True)
    fs[0] = jnp.broadcast_to(fsum, (8, BS))

    def fy_copy(o):
        return remote(fs.at[0], fy.at[o - 1], fy_s.at[o - 1], fy_r.at[o - 1], ydev(o))

    fz_copy = remote(fs.at[1], fz, fz_s.at[0], fz_r.at[0], zpartner)

    def fm_copy(d):
        return remote(fmr.at[0], fmr.at[d], fm_s.at[d], fm_r.at[d], fwrap(-d))

    for o in (1, 2, 3):
        fy_copy(o).start()
    single_product(aw, a, 0)
    y_start(m_self)
    for o in (1, 2, 3):
        fy_copy(o).wait_recv()
    fs[1] = (fs[0] + fy[0]) + (fy[1] + fy[2])
    fz_copy.start()

    def step_extra(core_index):
        @pl.when(c == core_index)
        def _():
            for t in range(T):
                ce_copy(t, a).wait_recv()
            single_product(aw, ex, 1)
            y_start(m_ex)

    arrive_early(0)
    step_early(0)
    step_extra(0)
    arrive_early(1)
    step_early(1)
    arrive_early(2)
    send_late()
    step_early(2)
    forward_late(0)
    forward_late(1)
    arrive_early(3)
    forward_late(2)
    step_early(3)
    forward_late(3)
    fz_copy.wait_recv()
    fmr[0] = (fs[1] + fz[...]) / total_pix
    for d in range(1, BAND):
        fm_copy(d).start()
    arrive_late(0)
    step_late(0)
    for t in range(T):
        send_extra(t)
    arrive_late(1)
    step_late(1)
    step_extra(1)
    z_start(m_self)
    z_start(m_early)
    arrive_late(2)
    step_late(2)
    z_start(m_early + 1)
    z_start(m_early + 2)

    for d in range(1, BAND):
        fm_copy(d).wait_recv()
    fcol[...] = jnp.transpose(jnp.broadcast_to(fmr[0, 0:1, :], (128, BS)))
    left = 1.0 / (fcol[pl.ds(pl.multiple_of(p * SH, SH), SH), :] * total_pix)
    left = jnp.concatenate([left] * (BS // 128), axis=1)

    def put(lag, v):
        v = v * left * (1.0 / fmr[lag, 0:1, :])
        out[:, lag, :] = jnp.where(f + lag < nf, v, 0.0)

    arrive_late(3)
    step_late(3)
    z_start(m_early + 3)
    z_start(m_late)
    far_home(0)
    z_start(m_late + 1)
    far_home(1)
    z_start(m_ex)
    z_copy(m_self).wait_recv()
    put(0, zo[0] + zr[0])
    z_start(m_late + 2)
    far_home(2)
    z_copy(m_ex).wait_recv()

    @pl.when(c == 0)
    def _():
        put(1, zo[1] + zr[1])

    @pl.when(c == 1)
    def _():
        put(7, zo[1] + zr[1])

    z_start(m_late + 3)
    far_home(3)
    for t in range(T):
        z_copy(m_early + t).wait_recv()
        z_copy(m_late + t).wait_recv()

    def put_pairs(base):
        for j in range(2):
            put(base[0] + j, natural(zo[2 + j] + zr[2 + j]))
            put(base[1] + j, natural(zo[4 + j] + zr[4 + j]))

    @pl.when(c == 0)
    def _():
        put_pairs((2, 6))

    @pl.when(c == 1)
    def _():
        put_pairs((1, 5))

    for t in range(T):
        for w in range(2):
            remote(hs.at[0, :, :, pl.ds(0, CR)], hb.at[w, :, :, pl.ds(0, CR)], hs_s.at[t, 0], hb_r.at[w, t],
                   homes[0]).wait_recv()

    def put_far(base):
        for j in range(2):
            put(base + j, natural(hb[0, j] + hb[1, j]))

    @pl.when(c == 0)
    def _():
        put_far(4)

    @pl.when(c == 1)
    def _():
        put_far(3)

    @pl.when(c == 0)
    def _():
        for t in range(T):
            x_copy(t).wait_send()

    for t in range(T):
        e_copy(t).wait_send()
        l_copy(t, a, core).wait_send()
        ce_copy(t, a).wait_send()
        for e in range(2):
            c_copy(e, t).wait_send()
        for h in range(2):
            home_copy(t, h, pl.ds(0, SH), pl.ds(0, CR)).wait_send()
        for o in (1, 2, 3):
            far_cols(t, o).wait_send()
    for copy in cs_copies:
        copy.wait_send()
    for o in (1, 2, 3):
        fy_copy(o).wait_send()
    fz_copy.wait_send()
    for d in range(1, BAND):
        fm_copy(d).wait_send()
    for m in range(len(messages)):
        for o in (1, 2, 3):
            y_copy(m, o).wait_send()
        z_copy(m).wait_send()


def on_device(frames, dark):
    n, pix = frames.shape
    total_frames = n * lax.axis_size("frame")
    total_pix = pix * lax.axis_size("pix")
    nm = 2 + 3 * T
    nz = 2 + 2 * T
    dma = pltpu.SemaphoreType.DMA
    vm = pltpu.VMEM
    block = (8, SH, pix)
    out = pl.pallas_call(
        functools.partial(kernel, float(total_frames), float(total_pix)),
        out_shape=jax.ShapeDtypeStruct((SH, BAND, BS), F32),
        in_specs=[pl.BlockSpec(memory_space=pl.ANY), pl.BlockSpec(memory_space=pltpu.VMEM)],
        out_specs=pl.BlockSpec(memory_space=pltpu.VMEM),
        scratch_shapes=[
            vm((BS, pix), F32), vm(block, BF16), vm(block, BF16), vm(block, BF16), vm(block, BF16),
            vm((2, T, 2, 8, CS, pix), BF16), vm(block, BF16), vm((CR, pix), BF16),
            vm((8, 2, 4, SH, BS), F32), vm((3, 8, 2, SH, BS), F32),
            vm((6, SH, BS), F32), vm((6, SH, BS), F32), vm((6, SH, BS), F32),
            vm((2, 2, SH, BS), F32), vm((2, 2, SH, BS), F32),
            vm((2, 8, pix // 8), F32), vm((10, 8, pix // 8), F32), vm((8, pix), F32),
            vm((2, 8, BS), F32), vm((3, 8, BS), F32), vm((8, BS), F32), vm((BAND, 8, BS), F32), vm((BS, 128), F32),
            dma((4,)),
            dma((T,)), dma((T,)), dma((T,)), dma((T,)), dma((T,)), dma((T,)),
            dma((T,)), dma((T,)), dma((2, T)), dma((2, T)),
            dma((nm, 3)), dma((nm, 3)), dma((nz,)), dma((nz,)), dma((T, 2)), dma((2, T)),
            dma((10,)), dma((10,)), dma((3,)), dma((3,)), dma((1,)), dma((1,)), dma((BAND,)), dma((BAND,)),
        ],
        compiler_params=pltpu.CompilerParams(
            collective_id=0, has_side_effects=True, vmem_limit_bytes=56 * 1024 * 1024),
        cost_estimate=pl.CostEstimate(flops=2 * 8 * BS * BS * pix, bytes_accessed=6 * BS * pix, transcendentals=0),
    )(frames, dark.reshape(1, pix))
    return out.reshape(SH, 1, BAND, BS)


def solution(mesh):
    return jax.shard_map(
        on_device,
        mesh=mesh,
        in_specs=(P("frame", "pix"), P("pix")),
        out_specs=P("pix", "frame", None, None),
        check_vma=False,
    )
```

```python
import functools

import jax
import jax.numpy as jnp
from jax import lax
from jax.experimental import pallas as pl
from jax.experimental.pallas import tpu as pltpu
from jax.sharding import PartitionSpec as P

BS = 512
SH = 64
T = 4
CS = SH // T
CR = BS // T
BAND = 8
F32 = jnp.float32
BF16 = jnp.bfloat16
MESH = pl.DeviceIdType.MESH


def nt_dot(left, right):
    return lax.dot_general(left, right, (((1,), (1,)), ((), ())), preferred_element_type=F32)


def natural(v):
    lane = lax.broadcasted_iota(jnp.int32, (v.shape[0], CR), 1)
    groups = []
    for g in range(BS // CR):
        acc = None
        for t in range(T):
            src = v[:, t * CR:(t + 1) * CR]
            for h in range(2):
                shift = (h * SH + t * CS) - (2 * g + h) * CS
                piece = pltpu.roll(src, shift % CR, 1) if shift % CR else src
                if acc is None:
                    acc = piece
                else:
                    start = h * SH + t * CS
                    acc = jnp.where((lane >= start) & (lane < start + CS), piece, acc)
        groups.append(acc)
    return jnp.concatenate(groups, axis=1)


def kernel(total_frames, total_pix, frames, dark, out,
           fr, a, aw, ap, ex, rv, nw, lw, ys, yr, zs, zo, zr, hs, hb,
           cs, cr, winv, fs, fy, fz, fmr, fcol,
           fl_s, x_s, x_r, e_s, e_r, l_s, l_r, ce_s, ce_r, c_s, c_r,
           ys_s, ys_r, zs_s, zs_r, hs_s, hb_r, cs_s, cs_r, fy_s, fy_r, fz_s, fz_r, fm_s, fm_r):
    f = lax.axis_index("frame")
    p = lax.axis_index("pix")
    nf = 32
    pix = fr.shape[1]
    c = lax.rem(f, 2)
    k = f // 2
    z = lax.rem(k, 4)
    x = k // 4
    y = lax.rem(p, 4)
    zl = p // 4

    def fdev(nx_, nz_, nc_):
        return ((nx_ * 4 + nz_) * 2 + nc_, p)

    def kdev(d):
        return (lax.rem(k + d, 16) * 2 + c, p)

    def fwrap(d):
        return (lax.rem(f + d + nf, nf), p)

    def zdev(o):
        return fdev(x, lax.rem(z + o, 4), c)

    def xdev(o):
        return fdev(lax.rem(x + o, 4), z, c)

    def ydev(o):
        return (f, zl * 4 + lax.rem(y + o, 4))

    core = fdev(x, z, 1 - c)
    zpartner = (f, (1 - zl) * 4 + y)
    plane = [core] + [fdev(x, lax.rem(z + o, 4), cc) for o in (1, 2, 3) for cc in (c, 1 - c)]
    homes = [(lax.rem(f + 2, nf), h * 4 + y) for h in range(2)]

    barrier = pltpu.get_barrier_semaphore()
    greet = [zpartner] + plane
    greet += [xdev(o) for o in (1, 2, 3)]
    greet += [ydev(o) for o in (1, 2, 3)]
    greet += [fwrap(d) for d in range(1, 8)]
    greet += [(lax.rem(f + nf - 2, nf), h * 4 + y) for h in range(2)]
    greet += [kdev(3 - 2 * zl), kdev(1 + 2 * zl)]
    for g in greet:
        pl.semaphore_signal(barrier, inc=1, device_id=g, device_id_type=MESH)

    rows = BS // 4
    loads = [pltpu.make_async_copy(frames.at[pl.ds(q * rows, rows)], fr.at[pl.ds(q * rows, rows)], fl_s.at[q])
             for q in range(4)]
    for ld in loads:
        ld.start()

    def remote(src, dst, s, r, dev):
        return pltpu.make_async_remote_copy(
            src_ref=src, dst_ref=dst, send_sem=s, recv_sem=r, device_id=dev, device_id_type=MESH)

    def part(ref, t):
        return ref.at[:, pl.ds(t * CS, CS), :]

    def x_copy(t):
        return remote(part(a, t), part(ap, t), x_s.at[t], x_r.at[t], xdev(3))

    def e_copy(t):
        return remote(part(a, t), rv.at[0, t, c], e_s.at[t], e_r.at[t], kdev(13 + 2 * zl))

    def l_copy(t, src, dev):
        return remote(part(src, t), rv.at[1, t, c], l_s.at[t], l_r.at[t], dev)

    def ce_copy(t, src):
        return remote(part(src, t), part(ex, t), ce_s.at[t], ce_r.at[t], core)

    def c_copy(e, t):
        return remote(rv.at[e, t, c], rv.at[e, t, c], c_s.at[e, t], c_r.at[e, t], core)

    dk = dark[0:1, :]
    colsum = None
    for q in range(4):
        loads[q].wait()
        sig = fr[q * rows:(q + 1) * rows, :] - dk
        a[2 * q:2 * q + 2] = sig.astype(BF16).reshape(2, SH, pix)
        partial = jnp.sum(sig, axis=0, keepdims=True)
        colsum = partial if colsum is None else colsum + partial

    width = pix // 8
    for i in range(8):
        cs[0, i:i + 1, :] = colsum[:, i * width:(i + 1) * width]

    def cs_copy(stage, i, dev):
        return remote(cs.at[stage], cr.at[i], cs_s.at[i], cs_r.at[i], dev)

    pl.semaphore_wait(barrier, len(greet))
    cs_copies = [cs_copy(0, i, d) for i, d in enumerate(plane)]
    cs_copies += [cs_copy(1, 6 + o, xdev(o)) for o in (1, 2, 3)]
    for copy in cs_copies[:7]:
        copy.start()
    along = z >= 3 - 2 * zl

    @pl.when(along)
    def _():
        for t in range(T):
            e_copy(t).start()

    for copy in cs_copies[:7]:
        copy.wait_recv()
    cs[1] = ((cs[0] + cr[0]) + (cr[1] + cr[2])) + ((cr[3] + cr[4]) + (cr[5] + cr[6]))
    for copy in cs_copies[7:]:
        copy.start()

    for t in range(T):
        @pl.when(jnp.logical_not(along))
        def _():
            e_copy(t).start()

        @pl.when(c == 0)
        def _():
            x_copy(t).start()

    @pl.when(c == 1)
    def _():
        for t in range(T):
            ce_copy(t, a).start()

    for copy in cs_copies[7:]:
        copy.wait_recv()
    pixel_mean = ((cs[1] + cr[7]) + (cr[8] + cr[9])) / total_frames
    inv8 = 1.0 / pixel_mean
    for i in range(8):
        winv[0:1, i * width:(i + 1) * width] = inv8[i:i + 1, :]

    def scaled(v):
        w = winv[0:1, :] * winv[0:1, :]
        return (v.astype(F32) * w).astype(BF16)

    early = 4 - 2 * zl
    late = 2 + 2 * zl
    m_self, m_ex, m_early, m_late, m_far = 0, 1, 2, 2 + T, 2 + 2 * T
    messages = [(0, 0, 1, 0, BS), (1, 1, 1, 0, BS)]
    messages += [(m_early + t, early, 2, t * CR, CR) for t in range(T)]
    messages += [(m_late + t, late, 2, t * CR, CR) for t in range(T)]

    def y_copy(m, o):
        dst = lax.rem(y + o, 4)
        _, s0, ns, c0, nc = messages[m]
        return remote(
            ys.at[pl.ds(s0, ns), :, dst, :, pl.ds(c0, nc)], yr.at[o - 1, pl.ds(s0, ns), :, :, pl.ds(c0, nc)],
            ys_s.at[m, o - 1], ys_r.at[m, o - 1], ydev(o))

    def far_rows(t, o):
        dst = lax.rem(y + o, 4)
        return remote(
            ys.at[pl.ds(6, 2), :, dst, pl.ds(t * CS, CS), :], yr.at[o - 1, pl.ds(6, 2), :, pl.ds(t * CS, CS), :],
            ys_s.at[m_far + t, o - 1], ys_r.at[m_far + t, o - 1], ydev(o))

    def far_cols(t, o):
        dst = lax.rem(y + o, 4)
        return remote(
            ys.at[pl.ds(6, 2), :, dst, :, pl.ds(t * CR, CR)], yr.at[o - 1, pl.ds(6, 2), :, :, pl.ds(t * CR, CR)],
            ys_s.at[m_far + t, o - 1], ys_r.at[m_far + t, o - 1], ydev(o))

    def y_start(m):
        for o in (2, 1, 3):
            y_copy(m, o).start()

    def z_copy(m):
        _, s0, ns, c0, nc = messages[m]
        return remote(zs.at[pl.ds(s0, ns), :, pl.ds(c0, nc)], zr.at[pl.ds(s0, ns), :, pl.ds(c0, nc)],
                      zs_s.at[m], zs_r.at[m], zpartner)

    def total(s, h, r, q):
        return (ys[s, h, y, r, q] + yr[0, s, h, r, q]) + (yr[1, s, h, r, q] + yr[2, s, h, r, q])

    def z_sum(m):
        _, s0, ns, c0, nc = messages[m]
        for o in (1, 2, 3):
            y_copy(m, o).wait_recv()
        cols = pl.ds(c0, nc)
        for i in range(ns):
            zs[s0 + i, :, cols] = total(s0 + i, 1 - zl, slice(None), cols)
        for i in range(ns):
            zo[s0 + i, :, cols] = total(s0 + i, zl, slice(None), cols)

    def z_start(m):
        z_sum(m)
        z_copy(m).start()

    def home_copy(t, h, r, q):
        return remote(hs.at[h, :, r, q], hb.at[zl, :, r, q], hs_s.at[t, h], hb_r.at[zl, t], homes[h])

    def far_sum(t):
        @pl.when(zl == 0)
        def _():
            r, q = pl.ds(t * CS, CS), pl.ds(0, BS)
            for o in (1, 2, 3):
                far_rows(t, o).wait_recv()
            for h in range(2):
                for j in range(2):
                    hs[h, j, r, :] = total(6 + j, h, r, q)

        @pl.when(zl == 1)
        def _():
            r, q = pl.ds(0, SH), pl.ds(t * CR, CR)
            for o in (1, 2, 3):
                far_cols(t, o).wait_recv()
            for h in range(2):
                for j in range(2):
                    hs[h, j, :, q] = total(6 + j, h, r, q)

    def far_send(t):
        @pl.when(zl == 0)
        def _():
            for h in range(2):
                home_copy(t, h, pl.ds(t * CS, CS), pl.ds(0, BS)).start()

        @pl.when(zl == 1)
        def _():
            for h in range(2):
                home_copy(t, h, pl.ds(0, SH), pl.ds(t * CR, CR)).start()

    def far_home(t):
        far_sum(t)
        far_send(t)

    def pair_product(left, e, s0, t):
        right = rv[e, t].reshape(2 * CR, pix)
        for h in range(2):
            prod = nt_dot(left[4 * h:4 * h + 4].reshape(4 * SH, pix), right)
            for j in range(2):
                ys[s0 + j, h, :, :, t * CR:(t + 1) * CR] = prod[:, j * CR:(j + 1) * CR].reshape(4, SH, CR)

    def single_product(left, right, s):
        for h in range(2):
            for q in range(2):
                prod = nt_dot(left[4 * h:4 * h + 4].reshape(4 * SH, pix), right[4 * q:4 * q + 4].reshape(4 * SH, pix))
                ys[s, h, :, :, q * 256:(q + 1) * 256] = prod.reshape(4, SH, 256)

    def far_product(t):
        @pl.when(zl == 0)
        def _():
            lw[...] = scaled(rv[1, t, c].reshape(CR, pix))
            for q in range(T):
                prod = nt_dot(lw[...], rv[0, q].reshape(2 * CR, pix))
                for j in range(2):
                    ys[6 + j, :, :, t * CS:(t + 1) * CS, q * CR:(q + 1) * CR] = (
                        prod[:, j * CR:(j + 1) * CR].reshape(2, 4, CS, CR))
            for o in (2, 1, 3):
                far_rows(t, o).start()

        @pl.when(zl == 1)
        def _():
            pair_product(nw, 1, 6, t)
            for o in (2, 1, 3):
                far_cols(t, o).start()

    def arrive_early(t):
        e_copy(t).wait_recv()
        c_copy(0, t).start()

    def step_early(t):
        c_copy(0, t).wait_recv()
        pair_product(aw, 0, early, t)
        y_start(m_early + t)

        @pl.when(zl == 1)
        def _():
            nw[:, t * CS:(t + 1) * CS, :] = scaled(rv[0, t, c])

    forward = (c == 0) & (z <= 2 * zl)

    def send_late():
        @pl.when(jnp.logical_not(forward))
        def _():
            for t in range(T):
                l_copy(t, a, kdev(15 - 2 * zl)).start()

    def forward_late(t):
        @pl.when(forward)
        def _():
            x_copy(t).wait_recv()
            l_copy(t, ap, zdev(3 - 2 * zl)).start()

    def send_extra(t):
        @pl.when(c == 0)
        def _():
            @pl.when(jnp.logical_not(forward))
            def _():
                x_copy(t).wait_recv()

            ce_copy(t, ap).start()

    def arrive_late(t):
        l_copy(t, a, core).wait_recv()
        c_copy(1, t).start()

    def step_late(t):
        c_copy(1, t).wait_recv()
        far_product(t)
        pair_product(aw, 1, late, t)
        y_start(m_late + t)

    for q in range(4):
        aw[2 * q:2 * q + 2] = scaled(fr[q * rows:(q + 1) * rows, :] - dk).reshape(2, SH, pix)
    inv = winv[0:1, :]
    hi = inv.astype(BF16).astype(F32)
    row = lax.broadcasted_iota(jnp.int32, (16, pix), 0)
    mix = jnp.where(row == 0, hi, jnp.where(row == 1, inv - hi, 0.0)).astype(BF16)
    fsum = jnp.sum(nt_dot(mix, a[...].reshape(BS, pix)), axis=0, keepdims=True)
    fs[0] = jnp.broadcast_to(fsum, (8, BS))

    def fy_copy(o):
        return remote(fs.at[0], fy.at[o - 1], fy_s.at[o - 1], fy_r.at[o - 1], ydev(o))

    fz_copy = remote(fs.at[1], fz, fz_s.at[0], fz_r.at[0], zpartner)

    def fm_copy(d):
        return remote(fmr.at[0], fmr.at[d], fm_s.at[d], fm_r.at[d], fwrap(-d))

    for o in (1, 2, 3):
        fy_copy(o).start()
    single_product(aw, a, 0)
    y_start(m_self)
    for o in (1, 2, 3):
        fy_copy(o).wait_recv()
    fs[1] = (fs[0] + fy[0]) + (fy[1] + fy[2])
    fz_copy.start()

    def step_extra(core_index):
        @pl.when(c == core_index)
        def _():
            for t in range(T):
                ce_copy(t, a).wait_recv()
            single_product(aw, ex, 1)
            y_start(m_ex)

    arrive_early(0)
    step_early(0)
    step_extra(0)
    arrive_early(1)
    step_early(1)
    arrive_early(2)
    send_late()
    step_early(2)
    forward_late(0)
    forward_late(1)
    arrive_early(3)
    forward_late(2)
    step_early(3)
    forward_late(3)
    fz_copy.wait_recv()
    fmr[0] = (fs[1] + fz[...]) / total_pix
    for d in range(1, BAND):
        fm_copy(d).start()
    arrive_late(0)
    step_late(0)
    for t in range(T):
        send_extra(t)
    arrive_late(1)
    step_late(1)
    step_extra(1)
    z_start(m_self)
    z_start(m_early)
    arrive_late(2)
    step_late(2)
    z_start(m_early + 1)
    z_start(m_early + 2)

    for d in range(1, BAND):
        fm_copy(d).wait_recv()
    fcol[...] = jnp.transpose(jnp.broadcast_to(fmr[0, 0:1, :], (128, BS)))
    left = 1.0 / (fcol[pl.ds(pl.multiple_of(p * SH, SH), SH), :] * total_pix)
    left = jnp.concatenate([left] * (BS // 128), axis=1)

    def put(lag, v):
        v = v * left * (1.0 / fmr[lag, 0:1, :])
        out[:, lag, :] = jnp.where(f + lag < nf, v, 0.0)

    arrive_late(3)
    step_late(3)
    z_start(m_early + 3)
    far_home(0)
    z_start(m_late)
    far_home(1)
    z_start(m_late + 1)
    z_start(m_ex)
    z_copy(m_self).wait_recv()
    put(0, zo[0] + zr[0])
    far_home(2)
    z_start(m_late + 2)
    z_copy(m_ex).wait_recv()

    @pl.when(c == 0)
    def _():
        put(1, zo[1] + zr[1])

    @pl.when(c == 1)
    def _():
        put(7, zo[1] + zr[1])

    far_home(3)
    z_start(m_late + 3)
    for t in range(T):
        z_copy(m_early + t).wait_recv()
        z_copy(m_late + t).wait_recv()

    def put_pairs(base):
        for j in range(2):
            put(base[0] + j, natural(zo[2 + j] + zr[2 + j]))
            put(base[1] + j, natural(zo[4 + j] + zr[4 + j]))

    @pl.when(c == 0)
    def _():
        put_pairs((2, 6))

    @pl.when(c == 1)
    def _():
        put_pairs((1, 5))

    for t in range(T):
        for w in range(2):
            remote(hs.at[0, :, :, pl.ds(0, CR)], hb.at[w, :, :, pl.ds(0, CR)], hs_s.at[t, 0], hb_r.at[w, t],
                   homes[0]).wait_recv()

    def put_far(base):
        for j in range(2):
            put(base + j, natural(hb[0, j] + hb[1, j]))

    @pl.when(c == 0)
    def _():
        put_far(4)

    @pl.when(c == 1)
    def _():
        put_far(3)

    @pl.when(c == 0)
    def _():
        for t in range(T):
            x_copy(t).wait_send()

    for t in range(T):
        e_copy(t).wait_send()
        l_copy(t, a, core).wait_send()
        ce_copy(t, a).wait_send()
        for e in range(2):
            c_copy(e, t).wait_send()
        for h in range(2):
            home_copy(t, h, pl.ds(0, SH), pl.ds(0, CR)).wait_send()
        for o in (1, 2, 3):
            far_cols(t, o).wait_send()
    for copy in cs_copies:
        copy.wait_send()
    for o in (1, 2, 3):
        fy_copy(o).wait_send()
    fz_copy.wait_send()
    for d in range(1, BAND):
        fm_copy(d).wait_send()
    for m in range(len(messages)):
        for o in (1, 2, 3):
            y_copy(m, o).wait_send()
        z_copy(m).wait_send()


def on_device(frames, dark):
    n, pix = frames.shape
    total_frames = n * lax.axis_size("frame")
    total_pix = pix * lax.axis_size("pix")
    nm = 2 + 3 * T
    nz = 2 + 2 * T
    dma = pltpu.SemaphoreType.DMA
    vm = pltpu.VMEM
    block = (8, SH, pix)
    out = pl.pallas_call(
        functools.partial(kernel, float(total_frames), float(total_pix)),
        out_shape=jax.ShapeDtypeStruct((SH, BAND, BS), F32),
        in_specs=[pl.BlockSpec(memory_space=pl.ANY), pl.BlockSpec(memory_space=pltpu.VMEM)],
        out_specs=pl.BlockSpec(memory_space=pltpu.VMEM),
        scratch_shapes=[
            vm((BS, pix), F32), vm(block, BF16), vm(block, BF16), vm(block, BF16), vm(block, BF16),
            vm((2, T, 2, 8, CS, pix), BF16), vm(block, BF16), vm((CR, pix), BF16),
            vm((8, 2, 4, SH, BS), F32), vm((3, 8, 2, SH, BS), F32),
            vm((6, SH, BS), F32), vm((6, SH, BS), F32), vm((6, SH, BS), F32),
            vm((2, 2, SH, BS), F32), vm((2, 2, SH, BS), F32),
            vm((2, 8, pix // 8), F32), vm((10, 8, pix // 8), F32), vm((8, pix), F32),
            vm((2, 8, BS), F32), vm((3, 8, BS), F32), vm((8, BS), F32), vm((BAND, 8, BS), F32), vm((BS, 128), F32),
            dma((4,)),
            dma((T,)), dma((T,)), dma((T,)), dma((T,)), dma((T,)), dma((T,)),
            dma((T,)), dma((T,)), dma((2, T)), dma((2, T)),
            dma((nm, 3)), dma((nm, 3)), dma((nz,)), dma((nz,)), dma((T, 2)), dma((2, T)),
            dma((10,)), dma((10,)), dma((3,)), dma((3,)), dma((1,)), dma((1,)), dma((BAND,)), dma((BAND,)),
        ],
        compiler_params=pltpu.CompilerParams(
            collective_id=0, has_side_effects=True, vmem_limit_bytes=56 * 1024 * 1024),
        cost_estimate=pl.CostEstimate(flops=2 * 8 * BS * BS * pix, bytes_accessed=6 * BS * pix, transcendentals=0),
    )(frames, dark.reshape(1, pix))
    return out.reshape(SH, 1, BAND, BS)


def solution(mesh):
    return jax.shard_map(
        on_device,
        mesh=mesh,
        in_specs=(P("frame", "pix"), P("pix")),
        out_specs=P("pix", "frame", None, None),
        check_vma=False,
    )
```
